32 devices in a mesh: dp: 4 (over y, x), expert: 8 (over z, core).
Axes of the slice: x: 2, y: 2, z: 4, core: 2. Of those that a mesh axis runs over, the one named last changes fastest.
Arguments:
- tokens: bfloat16 [1024, 2048], P(('dp', 'expert')), may hold values from -6 to 6
- tangent: bfloat16 [1024, 2048], P(('dp', 'expert')), may hold values from -6 to 6
- norm_gain: float32 [2048], replicated, may hold values from 0.1 to 1.9
- router: bfloat16 [2048, 16], replicated, may hold values from -0.125 to 0.125
- w_gate: bfloat16 [16, 2048, 768], P('expert', 'dp'), may hold values from -0.125 to 0.125
- w_up: bfloat16 [16, 2048, 768], P('expert', 'dp'), may hold values from -0.125 to 0.125
- w_down: bfloat16 [16, 768, 2048], P('expert', None, 'dp'), may hold values from -0.21875 to 0.21875
- routes: int32 [1024, 8], P(('dp', 'expert')), may hold values from 0 to 15, all different within a row; in each aligned block of 32 rows (0 to 31, 32 to 63, ...) at most 32 rows name the same one
Outputs:
- tangent_image: float32 [1024, 2048], P(('dp', 'expert'))
- gram_image: float32 [1024, 2048], P(('dp', 'expert'))
The draws below stay inside these ranges and needn't reach their ends.
Inputs may be any that keep to these rules, and one draw needn't show every extreme that they name: `routes`: each row names 8 different experts. Within the rows of one device (aligned blocks of 32 rows) no expert is named more than 32 times, and in some such blocks an expert is named exactly 32 times.
All inputs are finite; a program needn't handle non-finite values.
Results may differ from the reference program's by a relative error of at most 0.013.
Values may be sent and summed in bfloat16 or wider, within the bound.
A program may use at most 128 MiB of HBM per device.

```python
import math
import jax
import jax.numpy as jnp
import numpy as np
from jax import lax

D = 2048
FF = 768
TOPK = 8
TOK_DEV = 32
EXPERTS = 16
TOKENS = 1024
CAP = 32


def levels(stream_key, shape, cuts, least, top_value):
    loudness = 1.0
    for position, parts in cuts:
        draws = jax.random.uniform(jax.random.fold_in(jax.random.fold_in(stream_key, 6), position), (parts,), jnp.float32, least / len(cuts), top_value / len(cuts))
        loudness = loudness * jnp.repeat(jnp.exp(draws), shape[position] // parts).reshape((-1,) + (1,) * (len(shape) - 1 - position))
    return loudness


def shared_out(stream_key, own, number, rows, number_of, top, bound, slope):
    order = jax.random.permutation(stream_key, number_of)
    packed, common = portions_of(number_of, rows * top, bound, slope, True), portions_of(number_of, rows * top, bound, slope, False)
    places = jnp.arange(number_of)

    def named(sizes, rotation):
        used = int((sizes > 0).sum())
        fixed = max(1, used // 4)
        moved = fixed + (places - fixed + rotation * (used - fixed)) % max(1, number_of - fixed)
        return jnp.zeros((number_of,), jnp.int32).at[order[jnp.where(places < fixed, places, moved)]].set(jnp.asarray(sizes, jnp.int32))

    sizes = jnp.where(number % 4 == 0, named(packed, number // 4), named(common, number - number // 4 - 1))
    mixed = jax.random.permutation(jax.random.fold_in(own, 3), number_of)
    donor, receiver = mixed[0:number_of // 2 * 2:2], mixed[1:number_of // 2 * 2:2]
    margin = jnp.minimum(sizes[donor] - 1, bound - sizes[receiver]) // 2
    margin = jnp.where((donor == order[0]) | (receiver == order[0]) | (sizes[receiver] == 0), 0, jnp.maximum(margin, 0))
    moved = jax.random.randint(jax.random.fold_in(own, 4), (number_of // 2,), 0, 1 << 20) % (margin + 1)
    sizes = sizes.at[donor].add(-moved).at[receiver].add(moved)
    items = jnp.searchsorted(jnp.cumsum(sizes), jnp.arange(rows * top), side="right").astype(jnp.int32)
    listing = items.reshape(top, rows).T
    listing = listing[jax.random.permutation(jax.random.fold_in(own, 1), rows)]
    rotation = jax.random.randint(jax.random.fold_in(own, 2), (rows, 1), 0, top)
    return jnp.take_along_axis(listing, (jnp.arange(top)[None, :] + rotation) % top, axis=1)


def portions_of(amount, total, reach, slope, full):
    portions = [(1 << 20) // math.isqrt(standing ** slope) + 1 for standing in range(1, amount + 1)]
    largest = reach if full else min(reach, max(-(-total // amount), total * portions[0] // sum(portions)))
    least = 1 if total - largest >= amount - 1 else 0
    given, spare = [largest] + [least] * (amount - 1), total - largest - least * (amount - 1)
    while spare > 0:
        movable = [i for i in range(1, amount) if given[i] < largest] or [i for i in range(1, amount) if given[i] < reach]
        pool, remaining = sum([portions[i] for i in movable]), spare
        for i in movable:
            more = min(reach - given[i], max(1, remaining * portions[i] // pool), spare)
            given[i] = given[i] + more
            spare = spare - more
    return np.array(given)


def scatter_about(stream_key, extent, scale, most, pieces=(), kind=jnp.bfloat16):
    loudness = levels(stream_key, extent, pieces, -0.22, 0.18) if pieces else 1.0
    result = jax.random.normal(stream_key, extent, jnp.float32) * scale * loudness
    return jnp.minimum(jnp.maximum(result, -most), most).astype(kind)


def setup_inputs(seed: int = 0) -> dict:
    key_list = jax.random.split(jax.random.key(seed), 9)
    tokens = scatter_about(key_list[0], (TOKENS, D), 1.0, 6.0, ((0, 32),))
    tangent = scatter_about(key_list[1], (TOKENS, D), 1.0, 6.0, ((0, 32),))
    norm_gain = jnp.clip(1.0 + 0.18 * jax.random.normal(key_list[2], (D,), jnp.float32), 0.1, 1.9)
    router = scatter_about(key_list[3], (D, EXPERTS), D ** -0.5, 0.125)
    w_gate = scatter_about(key_list[4], (EXPERTS, D, FF), D ** -0.5, 0.125, ((0, 8), (1, 4)))
    w_up = scatter_about(key_list[5], (EXPERTS, D, FF), D ** -0.5, 0.125, ((0, 8), (1, 4)))
    w_down = scatter_about(key_list[6], (EXPERTS, FF, D), FF ** -0.5, 0.21875, ((0, 8), (2, 4)))
    routes_keys = jax.random.split(jax.random.fold_in(key_list[7], 1), TOKENS // TOK_DEV)
    routes_turns = jax.random.permutation(jax.random.fold_in(key_list[7], 3), TOKENS // TOK_DEV)
    routes = jax.vmap(lambda own, number: shared_out(jax.random.fold_in(key_list[7], 2), own, number, TOK_DEV, EXPERTS, TOPK, CAP, 2))(routes_keys, routes_turns).reshape((TOKENS, TOPK))
    return dict(tokens=tokens, tangent=tangent, norm_gain=norm_gain, router=router, w_gate=w_gate, w_up=w_up, w_down=w_down, routes=routes)


eps_value = 1e-06

def pick_columns(table, routes):
    hits = routes[:, :, None] == jnp.arange(table.shape[1], dtype=jnp.int32)[None, None, :]
    return lax.optimization_barrier(jnp.sum(jnp.where(hits, table[:, None, :], jnp.zeros((), table.dtype)), axis=2))

def round_keep(values):
    return lax.optimization_barrier(values.astype(jnp.bfloat16)).astype(jnp.float32)

def reference(tokens, tangent, norm_gain, router, w_gate, w_up, w_down, routes):
    xfull = tokens.astype(jnp.float32)
    vfull = tangent.astype(jnp.float32)
    inv_rms = lax.rsqrt(lax.optimization_barrier(jnp.mean(xfull * xfull, axis=1, keepdims=True)) + eps_value)
    normed = (norm_gain * xfull * inv_rms).astype(jnp.bfloat16)
    cross_term = lax.optimization_barrier(jnp.mean(xfull * vfull, axis=1, keepdims=True))
    normed_tan = (norm_gain * (vfull * inv_rms - xfull * inv_rms ** 3 * cross_term)).astype(jnp.bfloat16)
    logits = jnp.dot(normed, router, preferred_element_type=jnp.float32)
    logit_tan = jnp.dot(normed_tan, router, preferred_element_type=jnp.float32)
    selected = pick_columns(logits, routes)
    sel_tan = pick_columns(logit_tan, routes)
    exp_sel = jnp.exp(selected)
    gate_prob = exp_sel / lax.optimization_barrier(jnp.sum(exp_sel, axis=1, keepdims=True))
    gate_tan = gate_prob * (sel_tan - lax.optimization_barrier(jnp.sum(gate_prob * sel_tan, axis=1, keepdims=True)))
    gate_b = gate_prob.astype(jnp.bfloat16)
    gate_tan_b = gate_tan.astype(jnp.bfloat16)
    pair_count = TOKENS * TOPK
    flat_ids = routes.reshape(-1).astype(jnp.int32)
    per_expert = TOKENS // TOK_DEV * CAP
    onehot = (flat_ids[:, None] == jnp.arange(EXPERTS, dtype=jnp.int32)[None, :]).astype(jnp.int32)
    slot_rank = lax.optimization_barrier(jnp.sum(onehot * jnp.cumsum(onehot, axis=0), axis=1)) - 1
    slot_table = jnp.full((EXPERTS * per_expert,), -1, jnp.int32)
    slot_table = slot_table.at[flat_ids * per_expert + slot_rank].set(jnp.arange(pair_count, dtype=jnp.int32))
    slot_table = slot_table.reshape(EXPERTS, per_expert)

    def expert_forward(w_g, w_u, index):
        slot_valid = index >= 0
        safe_pair = jnp.maximum(index, 0)
        tok_idx = safe_pair // TOPK
        which_k = safe_pair % TOPK
        rows_n = jnp.where(slot_valid[:, None], normed[tok_idx], jnp.zeros((), jnp.bfloat16))
        rows_t = jnp.where(slot_valid[:, None], normed_tan[tok_idx], jnp.zeros((), jnp.bfloat16))
        pre_gate = jnp.dot(rows_n, w_g, preferred_element_type=jnp.float32)
        pre_up = jnp.dot(rows_n, w_u, preferred_element_type=jnp.float32)
        gate_dot = jnp.dot(rows_t, w_g, preferred_element_type=jnp.float32)
        up_dot = jnp.dot(rows_t, w_u, preferred_element_type=jnp.float32)
        sig_gate = jax.nn.sigmoid(pre_gate)
        silu_gate = pre_gate * sig_gate
        slope_gate = sig_gate * (1.0 + pre_gate * (1.0 - sig_gate))
        hidden = silu_gate * pre_up
        hidden_tan = slope_gate * gate_dot * pre_up + silu_gate * up_dot
        return (slot_valid, tok_idx, which_k, pre_up, silu_gate, slope_gate, hidden, hidden_tan)

    def jvp_step(image, inputs):
        w_g, w_u, w_d, index = inputs
        slot_valid, tok_idx, which_k, pre_up, silu_gate, slope_gate, hidden, hidden_tan = expert_forward(w_g, w_u, index)
        gate_val = gate_b[tok_idx, which_k].astype(jnp.float32)[:, None]
        tan_val = gate_tan_b[tok_idx, which_k].astype(jnp.float32)[:, None]
        mixed_rows = (tan_val * hidden + gate_val * hidden_tan).astype(jnp.bfloat16)
        pair_image = round_keep(jnp.dot(mixed_rows, w_d, preferred_element_type=jnp.float32))
        image = image.at[tok_idx].add(jnp.where(slot_valid[:, None], pair_image, 0.0))
        return (image, None)
    image_zero = jnp.zeros((TOKENS, D), jnp.float32)
    tangent_image, unused = lax.scan(jvp_step, image_zero, (w_gate, w_up, w_down, slot_table))
    image_b = tangent_image.astype(jnp.bfloat16)

    def vjp_step(carry, inputs):
        expert_grad, gate_cot = carry
        w_g, w_u, w_d, index = inputs
        slot_valid, tok_idx, which_k, pre_up, silu_gate, slope_gate, hidden, hidden_tan = expert_forward(w_g, w_u, index)
        gate_val = gate_b[tok_idx, which_k].astype(jnp.float32)[:, None]
        rows_u = jnp.where(slot_valid[:, None], image_b[tok_idx], jnp.zeros((), jnp.bfloat16))
        back_hidden = jnp.dot(rows_u, w_d.T, preferred_element_type=jnp.float32)
        pair_cot = round_keep(lax.optimization_barrier(jnp.sum(back_hidden * hidden, axis=1)))
        scaled = gate_val * back_hidden
        grad_gate = (scaled * pre_up * slope_gate).astype(jnp.bfloat16)
        grad_up = (scaled * silu_gate).astype(jnp.bfloat16)
        pair_grad = jnp.dot(grad_gate, w_g.T, preferred_element_type=jnp.float32) + jnp.dot(grad_up, w_u.T, preferred_element_type=jnp.float32)
        pair_grad = round_keep(pair_grad)
        expert_grad = expert_grad.at[tok_idx].add(jnp.where(slot_valid[:, None], pair_grad, 0.0))
        gate_cot = gate_cot.at[tok_idx, which_k].add(jnp.where(slot_valid, pair_cot, 0.0))
        return ((expert_grad, gate_cot), None)
    carry_zero = (jnp.zeros((TOKENS, D), jnp.float32), jnp.zeros((TOKENS, TOPK), jnp.float32))
    (expert_grad, gate_cot), unused = lax.scan(vjp_step, carry_zero, (w_gate, w_up, w_down, slot_table))
    logit_grad = gate_prob * (gate_cot - lax.optimization_barrier(jnp.sum(gate_prob * gate_cot, axis=1, keepdims=True)))
    hits = routes[:, :, None] == jnp.arange(EXPERTS, dtype=jnp.int32)[None, None, :]
    column_grad = lax.optimization_barrier(jnp.sum(jnp.where(hits, logit_grad[:, :, None], 0.0), axis=1))
    router_grad = jnp.dot(column_grad, router.astype(jnp.float32).T, precision=lax.Precision.HIGHEST)
    pulled = norm_gain * (expert_grad + router_grad)
    gram_image = inv_rms * pulled - xfull * inv_rms ** 3 * lax.optimization_barrier(jnp.mean(pulled * xfull, axis=1, keepdims=True))
    return (tangent_image, gram_image)
```

```python
import jax
import jax.numpy as jnp
from jax import lax
from jax.experimental import pallas as pl
from jax.experimental.pallas import tpu as pltpu
from jax.sharding import PartitionSpec as P

eps_value = 1e-06


def pick_columns(table, routes):
    hits = routes[:, :, None] == jnp.arange(table.shape[1], dtype=jnp.int32)[None, None, :]
    return jnp.sum(jnp.where(hits, table[:, None, :], jnp.zeros((), table.dtype)), axis=2)


def on_device(tokens, tangent, norm_gain, router, w_gate, w_up, w_down, routes):
    tok_rows, topk = routes.shape
    model_width = tokens.shape[1]
    experts_all = router.shape[1]
    local_experts = w_gate.shape[0]
    groups = lax.axis_size("expert")
    capacity = 2 * tok_rows * topk // experts_all
    xfull = tokens.astype(jnp.float32)
    vfull = tangent.astype(jnp.float32)
    inv_rms = lax.rsqrt(jnp.mean(xfull * xfull, axis=1, keepdims=True) + eps_value)
    normed = (norm_gain * xfull * inv_rms).astype(jnp.bfloat16)
    cross_term = jnp.mean(xfull * vfull, axis=1, keepdims=True)
    normed_tan = (norm_gain * (vfull * inv_rms - xfull * inv_rms**3 * cross_term)).astype(
        jnp.bfloat16
    )
    logits = jnp.dot(normed, router, preferred_element_type=jnp.float32)
    logit_tan = jnp.dot(normed_tan, router, preferred_element_type=jnp.float32)
    selected = pick_columns(logits, routes)
    sel_tan = pick_columns(logit_tan, routes)
    exp_sel = jnp.exp(selected)
    gate_prob = exp_sel / jnp.sum(exp_sel, axis=1, keepdims=True)
    gate_tan = gate_prob * (sel_tan - jnp.sum(gate_prob * sel_tan, axis=1, keepdims=True))
    gate_b = gate_prob.astype(jnp.bfloat16)
    gate_tan_b = gate_tan.astype(jnp.bfloat16)
    pair_count = tok_rows * topk
    flat_ids = routes.reshape(-1)
    order = jnp.arange(pair_count, dtype=jnp.int32)
    earlier = (flat_ids[None, :] == flat_ids[:, None]) & (order[None, :] < order[:, None])
    slot_rank = jnp.sum(earlier.astype(jnp.int32), axis=1)
    slot_of_pair = flat_ids * capacity + slot_rank
    slot_hits = slot_of_pair[None, :] == jnp.arange(experts_all * capacity, dtype=jnp.int32)[:, None]
    slot_table = jnp.max(
        jnp.where(slot_hits, jnp.arange(pair_count, dtype=jnp.int32)[None, :], -1), axis=1
    )
    slot_valid = slot_table >= 0
    safe_pair = jnp.maximum(slot_table, 0)
    tok_idx = safe_pair // topk
    which_k = safe_pair % topk
    bf_zero = jnp.zeros((), jnp.bfloat16)
    send_rows = jnp.stack(
        (
            jnp.where(slot_valid[:, None], normed[tok_idx], bf_zero),
            jnp.where(slot_valid[:, None], normed_tan[tok_idx], bf_zero),
        )
    )
    send_rows = send_rows.reshape(2, groups, local_experts * capacity, model_width)
    send_gates = jnp.stack(
        (
            jnp.where(slot_valid, gate_b[tok_idx, which_k], bf_zero),
            jnp.where(slot_valid, gate_tan_b[tok_idx, which_k], bf_zero),
        )
    )
    send_gates = send_gates.reshape(2, groups, local_experts * capacity)
    recv_rows, recv_gates = (
        lax.all_to_all(send_rows, "expert", split_axis=1, concat_axis=1, tiled=True),
        lax.all_to_all(send_gates, "expert", split_axis=1, concat_axis=1, tiled=True),
    )
    slot_rows = recv_rows.reshape(2, groups, local_experts, capacity, model_width)
    recv_gates = recv_gates.reshape(2, groups, local_experts, capacity).astype(jnp.float32)
    gate_val = recv_gates[0][..., None]
    tan_val = recv_gates[1][..., None]
    gate_full, up_full, down_full = (
        lax.all_gather(w_gate, "dp", axis=1, tiled=True),
        lax.all_gather(w_up, "dp", axis=1, tiled=True),
        lax.all_gather(w_down, "dp", axis=2, tiled=True),
    )
    pre_both = jnp.einsum(
        "tslkd,ldf->tslkf", slot_rows, gate_full, preferred_element_type=jnp.float32
    )
    up_both = jnp.einsum("tslkd,ldf->tslkf", slot_rows, up_full, preferred_element_type=jnp.float32)
    pre_gate = pre_both[0]
    gate_dot = pre_both[1]
    pre_up = up_both[0]
    up_dot = up_both[1]
    sig_gate = jax.nn.sigmoid(pre_gate)
    silu_gate = pre_gate * sig_gate
    slope_gate = sig_gate * (1.0 + pre_gate * (1.0 - sig_gate))
    hidden = silu_gate * pre_up
    hidden_tan = slope_gate * gate_dot * pre_up + silu_gate * up_dot
    mixed_rows = (tan_val * hidden + gate_val * hidden_tan).astype(jnp.bfloat16)
    pair_image = jnp.einsum(
        "slkf,lfd->slkd", mixed_rows, down_full, preferred_element_type=jnp.float32
    )
    pair_send = pair_image.astype(jnp.bfloat16).reshape(
        groups, local_experts * capacity, model_width
    )
    pair_back = lax.all_to_all(pair_send, "expert", split_axis=0, concat_axis=0, tiled=True)
    pair_back = pair_back.reshape(experts_all * capacity, model_width)
    tangent_image = jnp.sum(
        pair_back[slot_of_pair].astype(jnp.float32).reshape(tok_rows, topk, model_width), axis=1
    )
    image_b = tangent_image.astype(jnp.bfloat16)
    send_cot = jnp.where(slot_valid[:, None], image_b[tok_idx], bf_zero).reshape(
        groups, local_experts * capacity, model_width
    )
    recv_cot = lax.all_to_all(send_cot, "expert", split_axis=0, concat_axis=0, tiled=True)
    recv_cot = recv_cot.reshape(groups, local_experts, capacity, model_width)
    back_hidden = jnp.einsum(
        "slkd,lfd->slkf", recv_cot, down_full, preferred_element_type=jnp.float32
    )
    gate_cot = jnp.sum(back_hidden * hidden, axis=3).astype(jnp.bfloat16)
    scaled = gate_val * back_hidden
    grad_gate = (scaled * pre_up * slope_gate).astype(jnp.bfloat16)
    grad_up = (scaled * silu_gate).astype(jnp.bfloat16)
    pair_grad = jnp.einsum(
        "slkf,ldf->slkd", grad_gate, gate_full, preferred_element_type=jnp.float32
    )
    pair_grad = pair_grad + jnp.einsum(
        "slkf,ldf->slkd", grad_up, up_full, preferred_element_type=jnp.float32
    )
    grad_send = pair_grad.astype(jnp.bfloat16).reshape(
        groups, local_experts * capacity, model_width
    )
    cot_send = gate_cot.reshape(groups, local_experts * capacity)
    grad_back, cot_back = (
        lax.all_to_all(grad_send, "expert", split_axis=0, concat_axis=0, tiled=True),
        lax.all_to_all(cot_send, "expert", split_axis=0, concat_axis=0, tiled=True),
    )
    grad_back = grad_back.reshape(experts_all * capacity, model_width)
    cot_back = cot_back.reshape(experts_all * capacity)
    expert_grad = jnp.sum(
        grad_back[slot_of_pair].astype(jnp.float32).reshape(tok_rows, topk, model_width), axis=1
    )
    pair_cot = cot_back[slot_of_pair].astype(jnp.float32).reshape(tok_rows, topk)
    logit_grad = gate_prob * (pair_cot - jnp.sum(gate_prob * pair_cot, axis=1, keepdims=True))
    hits = routes[:, :, None] == jnp.arange(experts_all, dtype=jnp.int32)[None, None, :]
    column_grad = jnp.sum(jnp.where(hits, logit_grad[:, :, None], 0.0), axis=1)
    router_grad = jnp.dot(
        column_grad, router.astype(jnp.float32).T, precision=lax.Precision.HIGHEST
    )
    pulled = norm_gain * (expert_grad + router_grad)
    gram_image = inv_rms * pulled - xfull * inv_rms**3 * jnp.mean(
        pulled * xfull, axis=1, keepdims=True
    )
    return (tangent_image, gram_image)


MESH = pl.DeviceIdType.MESH
SHIFTS = [(dx, dz) for dx in range(2) for dz in range(4) if dx or dz]


def nt_dot(left, right):
    return lax.dot_general(
        left, right, (((1,), (1,)), ((), ())), preferred_element_type=jnp.float32
    )


def block_kernel(
    tok_ref, tan_ref, gain_ref, router_ref, routes_ref, wg_ref, wu_ref, wd_ref,
    image_ref, gram_ref,
    wgu, wd, rows, pre, mix, part, cross, summed, landed, image_rows,
    grads, part2, cross2, summed2, landed2, prob_keep, inv_keep,
    w_send, w_recv, w_own, a_send, a_recv, r_send, r_recv, c_send, c_recv,
):
    f32, bf = jnp.float32, jnp.bfloat16
    n_tok, width = tok_ref.shape
    slab, hid = wg_ref.shape[1], wg_ref.shape[2]
    half = hid // 2
    dp, ex = lax.axis_index("dp"), lax.axis_index("expert")
    y, x = dp // 2, dp % 2
    z, core = ex // 2, ex % 2
    other = 1 - core
    slot = x * 4 + z
    slot_rows = pl.ds(pl.multiple_of(slot * n_tok, n_tok), n_tok)
    mate = (dp, z * 2 + other)

    def same_core(dx, dz):
        return (y * 2 + (x + dx) % 2, (z + dz) % 4 * 2 + core)

    def same_slot(dx, dz):
        return (x + dx) % 2 * 4 + (z + dz) % 4

    plane = [(0, 1), (1, 0), (1, 1)]

    def in_plane(my, mx):
        return ((y + my) % 2 * 2 + (x + mx) % 2, ex)

    barrier = pltpu.get_barrier_semaphore()
    friends = [same_core(dx, dz) for dx, dz in SHIFTS] + [mate, in_plane(1, 0), in_plane(1, 1)]
    for friend in friends:
        pl.semaphore_signal(barrier, inc=1, device_id=friend, device_id_type=MESH)
    pl.semaphore_wait(barrier, len(friends))

    slab_rows = pl.ds(pl.multiple_of(dp * slab, slab), slab)

    def weight_ends(kind, l, to_x):
        cols = pl.ds(pl.multiple_of(to_x * half, half), half)
        if kind == 0:
            return wg_ref.at[l, :, cols], wgu.at[l, slab_rows, pl.ds(0, half)]
        if kind == 1:
            return wu_ref.at[l, :, cols], wgu.at[l, slab_rows, pl.ds(half, half)]
        return wd_ref.at[l, cols, :], wd.at[pl.ds(l * half, half), slab_rows]

    moving = {}

    def start_weights(kind, l):
        copies = []
        for p, (my, mx) in enumerate(plane):
            src, dst = weight_ends(kind, l, (x + mx) % 2)
            copies.append(
                pltpu.make_async_remote_copy(
                    src_ref=src, dst_ref=dst,
                    send_sem=w_send.at[kind, l, p], recv_sem=w_recv.at[kind, l, p],
                    device_id=in_plane(my, mx), device_id_type=MESH,
                )
            )
        for copy in copies:
            copy.start()
        src, dst = weight_ends(kind, l, x)
        own = pltpu.make_async_copy(src, dst, w_own.at[kind, l])
        own.start()
        moving[kind, l] = (copies, own)

    def need_weights(kind, l):
        copies, own = moving[kind, l]
        own.wait()
        for copy in copies:
            copy.wait_recv()

    def spread(buf, turn):
        copies = []
        for i, (dx, dz) in enumerate(SHIFTS):
            copies.append(
                pltpu.make_async_remote_copy(
                    src_ref=buf.at[core, slot_rows], dst_ref=buf.at[core, slot_rows],
                    send_sem=a_send.at[turn, i], recv_sem=a_recv.at[turn, i],
                    device_id=same_core(dx, dz), device_id_type=MESH,
                )
            )
        for copy in copies:
            copy.start()
        return copies

    def to_mate(src, dst, turn):
        copy = pltpu.make_async_remote_copy(
            src_ref=src, dst_ref=dst, send_sem=c_send.at[turn], recv_sem=c_recv.at[turn],
            device_id=mate, device_id_type=MESH,
        )
        copy.start()
        return copy

    def send_home(own_part, from_mate, out, land, turn):
        out[...] = (own_part.astype(f32) + from_mate.astype(f32)).astype(bf)
        copies = []
        for i, (dx, dz) in enumerate(SHIFTS):
            there = pl.ds(pl.multiple_of(same_slot(dx, dz) * n_tok, n_tok), n_tok)
            copies.append(
                pltpu.make_async_remote_copy(
                    src_ref=out.at[there], dst_ref=land.at[slot],
                    send_sem=r_send.at[turn, i], recv_sem=r_recv.at[turn, i],
                    device_id=same_core(dx, dz), device_id_type=MESH,
                )
            )
        for copy in copies:
            copy.start()
        land[slot] = out[slot_rows, :]
        for copy in copies:
            copy.wait_recv()
        total = land[0].astype(f32)
        for i in range(1, 8):
            total = total + land[i].astype(f32)
        return total, copies

    start_weights(0, 0)

    xfull = tok_ref[...].astype(f32)
    vfull = tan_ref[...].astype(f32)
    gain = gain_ref[...]
    inv_rms = lax.rsqrt(jnp.mean(xfull * xfull, axis=1, keepdims=True) + eps_value)
    normed = (gain * xfull * inv_rms).astype(bf)
    cross_term = jnp.mean(xfull * vfull, axis=1, keepdims=True)
    inv_cube = inv_rms * inv_rms * inv_rms
    normed_tan = (gain * (vfull * inv_rms - xfull * inv_cube * cross_term)).astype(bf)
    rows[core, slot_rows, 0:width] = normed
    rows[core, slot_rows, width : 2 * width] = normed_tan
    logits = jnp.dot(normed, router_ref[...], preferred_element_type=f32)
    logit_tan = jnp.dot(normed_tan, router_ref[...], preferred_element_type=f32)
    lanes = lax.broadcasted_iota(jnp.int32, (n_tok, 128), 1)
    chosen = jnp.zeros((n_tok, 128), f32)
    for k in range(routes_ref.shape[1]):
        chosen = chosen + jnp.where(lanes == routes_ref[:, k : k + 1], 1.0, 0.0)
    exp_sel = jnp.where(chosen > 0.5, jnp.exp(logits), 0.0)
    gate_prob = exp_sel / jnp.sum(exp_sel, axis=1, keepdims=True)
    gate_tan = gate_prob * (
        logit_tan - jnp.sum(gate_prob * logit_tan, axis=1, keepdims=True)
    )
    rows[core, slot_rows, 2 * width : 2 * width + 128] = gate_prob.astype(bf)
    rows[core, slot_rows, 2 * width + 128 : 2 * width + 256] = gate_tan.astype(bf)
    prob_keep[...] = gate_prob
    inv_keep[...] = jnp.broadcast_to(inv_rms, (n_tok, 128))

    sent = spread(rows, 0)
    pending = list(sent)
    start_weights(1, 0)
    start_weights(0, 1)
    start_weights(1, 1)
    start_weights(2, 0)
    start_weights(2, 1)
    for copy in sent:
        copy.wait_recv()
    copy = to_mate(rows.at[core], rows.at[core], 0)
    pending.append(copy)
    copy.wait_recv()

    n_rows = rows.shape[1]
    wide_lanes = lax.broadcasted_iota(jnp.int32, (n_rows, 128), 1)

    def gate_of(part_no, l, offset):
        table = rows[part_no, :, 2 * width + offset : 2 * width + offset + 128].astype(f32)
        return jnp.sum(jnp.where(wide_lanes == ex * 2 + l, table, 0.0), axis=1, keepdims=True)

    for l in range(2):
        need_weights(0, l)
        need_weights(1, l)

        @pl.loop(0, 2)
        def _(h):
            pre[l, h] = jnp.dot(rows[h, :, 0:width], wgu[l], preferred_element_type=f32)
            dots = jnp.dot(rows[h, :, width : 2 * width], wgu[l], preferred_element_type=f32)
            pre_gate, pre_up = pre[l, h, :, 0:half], pre[l, h, :, half:hid]
            gate_dot, up_dot = dots[:, 0:half], dots[:, half:hid]
            sig = jax.nn.sigmoid(pre_gate)
            silu = pre_gate * sig
            slope = sig * (1.0 + pre_gate * (1.0 - sig))
            hidden_tan = slope * gate_dot * pre_up + silu * up_dot
            mixed = gate_of(h, l, 128) * (silu * pre_up) + gate_of(h, l, 0) * hidden_tan
            mix[h, :, l * half : (l + 1) * half] = mixed.astype(bf)

    need_weights(2, 0)
    need_weights(2, 1)

    def down(part_no):
        part[part_no] = jnp.dot(mix[part_no], wd[...], preferred_element_type=f32).astype(bf)

    down(other)
    copy = to_mate(part.at[other], cross, 1)
    pending.append(copy)
    down(core)
    copy.wait_recv()
    image, sent = send_home(part[core], cross[...], summed, landed, 0)
    pending.extend(sent)
    image_ref[...] = image
    image_rows[core, slot_rows, :] = image.astype(bf)
    sent = spread(image_rows, 1)
    pending.extend(sent)
    for copy in sent:
        copy.wait_recv()
    copy = to_mate(image_rows.at[core], image_rows.at[core], 2)
    pending.append(copy)

    def backward(part_no):
        back = nt_dot(image_rows[part_no], wd[...])
        cots = jnp.zeros((n_rows, 128), f32)
        for l in range(2):
            back_hidden = back[:, l * half : (l + 1) * half]
            pre_gate, pre_up = pre[l, part_no, :, 0:half], pre[l, part_no, :, half:hid]
            sig = jax.nn.sigmoid(pre_gate)
            silu = pre_gate * sig
            slope = sig * (1.0 + pre_gate * (1.0 - sig))
            cot = jnp.sum(back_hidden * (silu * pre_up), axis=1, keepdims=True)
            cots = cots + jnp.where(wide_lanes == ex * 2 + l, cot, 0.0)
            scaled = gate_of(part_no, l, 0) * back_hidden
            grads[l, :, 0:half] = (scaled * pre_up * slope).astype(bf)
            grads[l, :, half:hid] = (scaled * silu).astype(bf)
        total = nt_dot(grads[0], wgu[0]) + nt_dot(grads[1], wgu[1])
        part2[part_no, :, 0:width] = total.astype(bf)
        part2[part_no, :, width : width + 128] = cots.astype(bf)

    backward(core)
    copy.wait_recv()
    backward(other)
    copy = to_mate(part2.at[other], cross2, 3)
    pending.append(copy)
    copy.wait_recv()
    total, sent = send_home(part2[core], cross2[...], summed2, landed2, 1)
    pending.extend(sent)

    expert_grad = total[:, 0:width]
    cot = total[:, width : width + 128]
    prob = prob_keep[...]
    column_grad = prob * (cot - jnp.sum(prob * cot, axis=1, keepdims=True))
    high = column_grad.astype(bf)
    rest = column_grad - high.astype(f32)
    middle = rest.astype(bf)
    low = (rest - middle.astype(f32)).astype(bf)
    router = router_ref[...]
    router_grad = nt_dot(high, router) + (nt_dot(middle, router) + nt_dot(low, router))
    xfull = tok_ref[...].astype(f32)
    inv_rms = inv_keep[:, 0:1]
    pulled = gain_ref[...] * (expert_grad + router_grad)
    gram_ref[...] = inv_rms * pulled - xfull * (inv_rms * inv_rms * inv_rms) * jnp.mean(
        pulled * xfull, axis=1, keepdims=True
    )
    for copy in pending:
        copy.wait_send()
    for copies, _ in moving.values():
        for copy in copies:
            copy.wait_send()


def on_device_dense(tokens, tangent, norm_gain, router, w_gate, w_up, w_down, routes):
    n_tok, width = tokens.shape
    hid = w_gate.shape[2]
    n_rows = 8 * n_tok
    bf, f32 = jnp.bfloat16, jnp.float32
    wide_router = jnp.pad(router, ((0, 0), (0, 128 - router.shape[1])))
    vm = pl.BlockSpec(memory_space=pltpu.VMEM)
    hbm = pl.BlockSpec(memory_space=pl.ANY)
    out = jax.ShapeDtypeStruct((n_tok, width), f32)
    dma = pltpu.SemaphoreType.DMA
    image, gram = pl.pallas_call(
        block_kernel,
        out_shape=(out, out),
        in_specs=[vm] * 5 + [hbm] * 3,
        out_specs=(vm, vm),
        scratch_shapes=[
            pltpu.VMEM((2, width, hid), bf),
            pltpu.VMEM((hid, width), bf),
            pltpu.VMEM((2, n_rows, 2 * width + 256), bf),
            pltpu.VMEM((2, 2, n_rows, hid), f32),
            pltpu.VMEM((2, n_rows, hid), bf),
            pltpu.VMEM((2, n_rows, width), bf),
            pltpu.VMEM((n_rows, width), bf),
            pltpu.VMEM((n_rows, width), bf),
            pltpu.VMEM((8, n_tok, width), bf),
            pltpu.VMEM((2, n_rows, width), bf),
            pltpu.VMEM((2, n_rows, hid), bf),
            pltpu.VMEM((2, n_rows, width + 128), bf),
            pltpu.VMEM((n_rows, width + 128), bf),
            pltpu.VMEM((n_rows, width + 128), bf),
            pltpu.VMEM((8, n_tok, width + 128), bf),
            pltpu.VMEM((n_tok, 128), f32),
            pltpu.VMEM((n_tok, 128), f32),
            dma((3, 2, 3)), dma((3, 2, 3)), dma((3, 2)),
            dma((2, 7)), dma((2, 7)), dma((2, 7)), dma((2, 7)), dma((4,)), dma((4,)),
        ],
        compiler_params=pltpu.CompilerParams(
            collective_id=0, has_side_effects=True, vmem_limit_bytes=56 * 2**20
        ),
        cost_estimate=pl.CostEstimate(
            flops=2 * 16 * n_rows * width * hid, bytes_accessed=2**24, transcendentals=2**20
        ),
    )(tokens, tangent, norm_gain.reshape(1, width), wide_router, routes, w_gate, w_up, w_down)
    return image, gram


def solution(mesh):
    in_specs = (
        P(("dp", "expert"), None),
        P(("dp", "expert"), None),
        P(),
        P(),
        P("expert", "dp", None),
        P("expert", "dp", None),
        P("expert", None, "dp"),
        P(("dp", "expert"), None),
    )
    out_specs = (P(("dp", "expert"), None), P(("dp", "expert"), None))
    body = on_device
    if mesh.shape["dp"] == 4 and mesh.shape["expert"] == 8:
        body = on_device_dense
    return jax.shard_map(
        body, mesh=mesh, in_specs=in_specs, out_specs=out_specs, check_vma=False
    )
```

```python
import jax
import jax.numpy as jnp
from jax import lax
from jax.experimental import pallas as pl
from jax.experimental.pallas import tpu as pltpu
from jax.sharding import PartitionSpec as P

eps_value = 1e-06


def pick_columns(table, routes):
    hits = routes[:, :, None] == jnp.arange(table.shape[1], dtype=jnp.int32)[None, None, :]
    return jnp.sum(jnp.where(hits, table[:, None, :], jnp.zeros((), table.dtype)), axis=2)


def on_device(tokens, tangent, norm_gain, router, w_gate, w_up, w_down, routes):
    tok_rows, topk = routes.shape
    model_width = tokens.shape[1]
    experts_all = router.shape[1]
    local_experts = w_gate.shape[0]
    groups = lax.axis_size("expert")
    capacity = 2 * tok_rows * topk // experts_all
    xfull = tokens.astype(jnp.float32)
    vfull = tangent.astype(jnp.float32)
    inv_rms = lax.rsqrt(jnp.mean(xfull * xfull, axis=1, keepdims=True) + eps_value)
    normed = (norm_gain * xfull * inv_rms).astype(jnp.bfloat16)
    cross_term = jnp.mean(xfull * vfull, axis=1, keepdims=True)
    normed_tan = (norm_gain * (vfull * inv_rms - xfull * inv_rms**3 * cross_term)).astype(
        jnp.bfloat16
    )
    logits = jnp.dot(normed, router, preferred_element_type=jnp.float32)
    logit_tan = jnp.dot(normed_tan, router, preferred_element_type=jnp.float32)
    selected = pick_columns(logits, routes)
    sel_tan = pick_columns(logit_tan, routes)
    exp_sel = jnp.exp(selected)
    gate_prob = exp_sel / jnp.sum(exp_sel, axis=1, keepdims=True)
    gate_tan = gate_prob * (sel_tan - jnp.sum(gate_prob * sel_tan, axis=1, keepdims=True))
    gate_b = gate_prob.astype(jnp.bfloat16)
    gate_tan_b = gate_tan.astype(jnp.bfloat16)
    pair_count = tok_rows * topk
    flat_ids = routes.reshape(-1)
    order = jnp.arange(pair_count, dtype=jnp.int32)
    earlier = (flat_ids[None, :] == flat_ids[:, None]) & (order[None, :] < order[:, None])
    slot_rank = jnp.sum(earlier.astype(jnp.int32), axis=1)
    slot_of_pair = flat_ids * capacity + slot_rank
    slot_hits = slot_of_pair[None, :] == jnp.arange(experts_all * capacity, dtype=jnp.int32)[:, None]
    slot_table = jnp.max(
        jnp.where(slot_hits, jnp.arange(pair_count, dtype=jnp.int32)[None, :], -1), axis=1
    )
    slot_valid = slot_table >= 0
    safe_pair = jnp.maximum(slot_table, 0)
    tok_idx = safe_pair // topk
    which_k = safe_pair % topk
    bf_zero = jnp.zeros((), jnp.bfloat16)
    send_rows = jnp.stack(
        (
            jnp.where(slot_valid[:, None], normed[tok_idx], bf_zero),
            jnp.where(slot_valid[:, None], normed_tan[tok_idx], bf_zero),
        )
    )
    send_rows = send_rows.reshape(2, groups, local_experts * capacity, model_width)
    send_gates = jnp.stack(
        (
            jnp.where(slot_valid, gate_b[tok_idx, which_k], bf_zero),
            jnp.where(slot_valid, gate_tan_b[tok_idx, which_k], bf_zero),
        )
    )
    send_gates = send_gates.reshape(2, groups, local_experts * capacity)
    recv_rows, recv_gates = (
        lax.all_to_all(send_rows, "expert", split_axis=1, concat_axis=1, tiled=True),
        lax.all_to_all(send_gates, "expert", split_axis=1, concat_axis=1, tiled=True),
    )
    slot_rows = recv_rows.reshape(2, groups, local_experts, capacity, model_width)
    recv_gates = recv_gates.reshape(2, groups, local_experts, capacity).astype(jnp.float32)
    gate_val = recv_gates[0][..., None]
    tan_val = recv_gates[1][..., None]
    gate_full, up_full, down_full = (
        lax.all_gather(w_gate, "dp", axis=1, tiled=True),
        lax.all_gather(w_up, "dp", axis=1, tiled=True),
        lax.all_gather(w_down, "dp", axis=2, tiled=True),
    )
    pre_both = jnp.einsum(
        "tslkd,ldf->tslkf", slot_rows, gate_full, preferred_element_type=jnp.float32
    )
    up_both = jnp.einsum("tslkd,ldf->tslkf", slot_rows, up_full, preferred_element_type=jnp.float32)
    pre_gate = pre_both[0]
    gate_dot = pre_both[1]
    pre_up = up_both[0]
    up_dot = up_both[1]
    sig_gate = jax.nn.sigmoid(pre_gate)
    silu_gate = pre_gate * sig_gate
    slope_gate = sig_gate * (1.0 + pre_gate * (1.0 - sig_gate))
    hidden = silu_gate * pre_up
    hidden_tan = slope_gate * gate_dot * pre_up + silu_gate * up_dot
    mixed_rows = (tan_val * hidden + gate_val * hidden_tan).astype(jnp.bfloat16)
    pair_image = jnp.einsum(
        "slkf,lfd->slkd", mixed_rows, down_full, preferred_element_type=jnp.float32
    )
    pair_send = pair_image.astype(jnp.bfloat16).reshape(
        groups, local_experts * capacity, model_width
    )
    pair_back = lax.all_to_all(pair_send, "expert", split_axis=0, concat_axis=0, tiled=True)
    pair_back = pair_back.reshape(experts_all * capacity, model_width)
    tangent_image = jnp.sum(
        pair_back[slot_of_pair].astype(jnp.float32).reshape(tok_rows, topk, model_width), axis=1
    )
    image_b = tangent_image.astype(jnp.bfloat16)
    send_cot = jnp.where(slot_valid[:, None], image_b[tok_idx], bf_zero).reshape(
        groups, local_experts * capacity, model_width
    )
    recv_cot = lax.all_to_all(send_cot, "expert", split_axis=0, concat_axis=0, tiled=True)
    recv_cot = recv_cot.reshape(groups, local_experts, capacity, model_width)
    back_hidden = jnp.einsum(
        "slkd,lfd->slkf", recv_cot, down_full, preferred_element_type=jnp.float32
    )
    gate_cot = jnp.sum(back_hidden * hidden, axis=3).astype(jnp.bfloat16)
    scaled = gate_val * back_hidden
    grad_gate = (scaled * pre_up * slope_gate).astype(jnp.bfloat16)
    grad_up = (scaled * silu_gate).astype(jnp.bfloat16)
    pair_grad = jnp.einsum(
        "slkf,ldf->slkd", grad_gate, gate_full, preferred_element_type=jnp.float32
    )
    pair_grad = pair_grad + jnp.einsum(
        "slkf,ldf->slkd", grad_up, up_full, preferred_element_type=jnp.float32
    )
    grad_send = pair_grad.astype(jnp.bfloat16).reshape(
        groups, local_experts * capacity, model_width
    )
    cot_send = gate_cot.reshape(groups, local_experts * capacity)
    grad_back, cot_back = (
        lax.all_to_all(grad_send, "expert", split_axis=0, concat_axis=0, tiled=True),
        lax.all_to_all(cot_send, "expert", split_axis=0, concat_axis=0, tiled=True),
    )
    grad_back = grad_back.reshape(experts_all * capacity, model_width)
    cot_back = cot_back.reshape(experts_all * capacity)
    expert_grad = jnp.sum(
        grad_back[slot_of_pair].astype(jnp.float32).reshape(tok_rows, topk, model_width), axis=1
    )
    pair_cot = cot_back[slot_of_pair].astype(jnp.float32).reshape(tok_rows, topk)
    logit_grad = gate_prob * (pair_cot - jnp.sum(gate_prob * pair_cot, axis=1, keepdims=True))
    hits = routes[:, :, None] == jnp.arange(experts_all, dtype=jnp.int32)[None, None, :]
    column_grad = jnp.sum(jnp.where(hits, logit_grad[:, :, None], 0.0), axis=1)
    router_grad = jnp.dot(
        column_grad, router.astype(jnp.float32).T, precision=lax.Precision.HIGHEST
    )
    pulled = norm_gain * (expert_grad + router_grad)
    gram_image = inv_rms * pulled - xfull * inv_rms**3 * jnp.mean(
        pulled * xfull, axis=1, keepdims=True
    )
    return (tangent_image, gram_image)


MESH = pl.DeviceIdType.MESH


def nt_dot(left, right):
    return lax.dot_general(
        left, right, (((1,), (1,)), ((), ())), preferred_element_type=jnp.float32
    )


def block_kernel(
    tok_ref, tan_ref, gain_ref, router_ref, routes_ref, wg_ref, wu_ref, wd_ref,
    image_ref, gram_ref,
    wgu, wd, rows, pre, mix, part, cross, summed, far, landed, image_rows,
    grads, part2, cross2, summed2, far2, landed2, prob_keep, inv_keep,
    w_send, w_recv, w_own, a_send, a_recv, r_send, r_recv, c_send, c_recv,
):
    f32, bf = jnp.float32, jnp.bfloat16
    n_tok, width = tok_ref.shape
    slab, hid = wg_ref.shape[1], wg_ref.shape[2]
    half = hid // 2
    n_core = 4 * n_tok
    dp, ex = lax.axis_index("dp"), lax.axis_index("expert")
    y, x = dp // 2, dp % 2
    z, core = ex // 2, ex % 2
    other = 1 - core
    x_peer = (y * 2 + 1 - x, ex)
    y_peer = ((1 - y) * 2 + x, ex)
    mate = (dp, z * 2 + other)
    z_peers = [(dp, (z + dz) % 4 * 2 + core) for dz in range(1, 4)]
    core_rows = pl.ds(pl.multiple_of(core * n_core, n_core), n_core)
    other_rows = pl.ds(pl.multiple_of(other * n_core, n_core), n_core)

    def block_rows(dz):
        return pl.ds(pl.multiple_of(core * n_core + (z + dz) % 4 * n_tok, n_tok), n_tok)

    def z_rows(dz):
        return pl.ds(pl.multiple_of((z + dz) % 4 * n_tok, n_tok), n_tok)

    slot_rows = block_rows(0)

    barrier = pltpu.get_barrier_semaphore()
    friends = z_peers + [x_peer, y_peer, mate]
    for friend in friends:
        pl.semaphore_signal(barrier, inc=1, device_id=friend, device_id_type=MESH)
    pl.semaphore_wait(barrier, len(friends))

    pending = []

    def push(src, dst, sems, where, device):
        copy = pltpu.make_async_remote_copy(
            src_ref=src, dst_ref=dst, send_sem=sems[0].at[where], recv_sem=sems[1].at[where],
            device_id=device, device_id_type=MESH,
        )
        copy.start()
        pending.append(copy)
        return copy

    def slab_of(index):
        return pl.ds(pl.multiple_of(index * slab, slab), slab)

    def weight_dst(kind, l, index):
        if kind == 2:
            return wd.at[pl.ds(l * half, half), slab_of(index)]
        return wgu.at[l, slab_of(index), pl.ds(kind * half, half)]

    def weight_src(kind, l, which):
        part_of = pl.ds(pl.multiple_of(which * half, half), half)
        if kind == 2:
            return wd_ref.at[l, part_of, :]
        return (wg_ref, wu_ref)[kind].at[l, :, part_of]

    moving, relayed = {}, {}
    w_sems = (w_send, w_recv)

    def start_weights(kind, l):
        mine = weight_dst(kind, l, dp)
        for_x, for_y = (1 - x, x) if l == 0 else (y, 1 - y)
        own = pltpu.make_async_copy(
            weight_src(kind, l, x if l == 0 else y), mine, w_own.at[kind, l]
        )
        ends = [(for_x, 0, x_peer), (for_y, 1, y_peer)]
        copies = [
            push(weight_src(kind, l, which), mine, w_sems, (kind, l, p), peer)
            for which, p, peer in ends
        ]
        own.start()
        moving[kind, l] = (copies, own)

    def relay_weights(kind, l):
        moving[kind, l][0][l].wait_recv()
        if l == 0:
            block = weight_dst(kind, l, y * 2 + 1 - x)
            relayed[kind, l] = push(block, block, w_sems, (kind, l, 2), y_peer)
        else:
            block = weight_dst(kind, l, (1 - y) * 2 + x)
            relayed[kind, l] = push(block, block, w_sems, (kind, l, 2), x_peer)

    def need_weights(kind, l):
        copies, own = moving[kind, l]
        own.wait()
        copies[1 - l].wait_recv()
        relayed[kind, l].wait_recv()

    a_sems, c_sems, r_sems = (a_send, a_recv), (c_send, c_recv), (r_send, r_recv)

    def gather_start(buf, turn):
        mine = buf.at[0, slot_rows]
        along_z = [
            push(mine, mine, a_sems, (turn, 0, i + 1), peer) for i, peer in enumerate(z_peers)
        ]
        sides = [
            [push(mine, buf.at[1 + s, slot_rows], a_sems, (turn, 1 + s, 0), peer)]
            for s, peer in enumerate((x_peer, y_peer))
        ]
        return along_z, sides

    def gather_finish(buf, turn, started):
        along_z, sides = started
        for dz in (3, 1, 2):
            along_z[dz - 1].wait_recv()
            got = block_rows(4 - dz)
            for s, peer in enumerate((x_peer, y_peer)):
                sides[s].append(
                    push(buf.at[0, got], buf.at[1 + s, got], a_sems, (turn, 1 + s, dz), peer)
                )
        to_mate = [push(buf.at[0, core_rows], buf.at[0, core_rows], c_sems, (turn, 0), mate)]
        for s in range(2):
            for copy in sides[s]:
                copy.wait_recv()
            block = buf.at[1 + s, core_rows]
            to_mate.append(push(block, block, c_sems, (turn, 1 + s), mate))
        return to_mate

    def send_home(compute, parts, crossed, mid, far, land, turn):
        over, aside = {}, []

        def to_mate(g):
            over[g] = push(
                parts.at[g, other_rows], crossed.at[g], c_sems, (2 + turn, g), mate
            )

        def add_mate(g):
            over[g].wait_recv()
            mid[g] = (parts[g, core_rows, :].astype(f32) + crossed[g].astype(f32)).astype(bf)

        def to_side(g, peer):
            add_mate(g)
            aside.append(push(mid.at[g], far.at[g - 1], r_sems, (turn, 3 + g), peer))

        compute(1)
        to_mate(1)
        compute(2)
        to_mate(2)
        to_side(1, x_peer)
        compute(0)
        to_mate(0)
        to_side(2, y_peer)
        over[0].wait_recv()
        for copy in aside:
            copy.wait_recv()
        own = parts[0, core_rows, :].astype(f32) + crossed[0].astype(f32)
        mid[0] = (own + (far[0].astype(f32) + far[1].astype(f32))).astype(bf)
        copies = [
            push(mid.at[0, z_rows(i + 1)], land.at[z], r_sems, (turn, 1 + i), peer)
            for i, peer in enumerate(z_peers)
        ]
        land[z] = mid[0, z_rows(0), :]
        for copy in copies:
            copy.wait_recv()
        return (land[0].astype(f32) + land[1].astype(f32)) + (
            land[2].astype(f32) + land[3].astype(f32)
        )

    start_weights(0, 0)

    xfull = tok_ref[...].astype(f32)
    vfull = tan_ref[...].astype(f32)
    gain = gain_ref[...]
    inv_rms = lax.rsqrt(jnp.mean(xfull * xfull, axis=1, keepdims=True) + eps_value)
    normed = (gain * xfull * inv_rms).astype(bf)
    cross_term = jnp.mean(xfull * vfull, axis=1, keepdims=True)
    inv_cube = inv_rms * inv_rms * inv_rms
    normed_tan = (gain * (vfull * inv_rms - xfull * inv_cube * cross_term)).astype(bf)
    rows[0, slot_rows, 0:width] = normed
    rows[0, slot_rows, width : 2 * width] = normed_tan
    logits = jnp.dot(normed, router_ref[...], preferred_element_type=f32)
    logit_tan = jnp.dot(normed_tan, router_ref[...], preferred_element_type=f32)
    lanes = lax.broadcasted_iota(jnp.int32, (n_tok, 128), 1)
    chosen = jnp.zeros((n_tok, 128), f32)
    for k in range(routes_ref.shape[1]):
        chosen = chosen + jnp.where(lanes == routes_ref[:, k : k + 1], 1.0, 0.0)
    exp_sel = jnp.where(chosen > 0.5, jnp.exp(logits), 0.0)
    gate_prob = exp_sel / jnp.sum(exp_sel, axis=1, keepdims=True)
    gate_tan = gate_prob * (
        logit_tan - jnp.sum(gate_prob * logit_tan, axis=1, keepdims=True)
    )
    rows[0, slot_rows, 2 * width : 2 * width + 128] = gate_prob.astype(bf)
    rows[0, slot_rows, 2 * width + 128 : 2 * width + 256] = gate_tan.astype(bf)
    prob_keep[...] = gate_prob
    inv_keep[...] = jnp.broadcast_to(inv_rms, (n_tok, 128))

    started = gather_start(rows, 0)
    pieces = [(0, 0), (1, 0), (0, 1), (1, 1), (2, 0), (2, 1)]
    for kind, l in pieces[1:]:
        start_weights(kind, l)
    for copy in gather_finish(rows, 0, started):
        copy.wait_recv()
    for kind, l in pieces:
        relay_weights(kind, l)

    n_rows = rows.shape[1]
    wide_lanes = lax.broadcasted_iota(jnp.int32, (n_rows, 128), 1)

    def gate_of(part_no, l, offset):
        table = rows[part_no, :, 2 * width + offset : 2 * width + offset + 128].astype(f32)
        return jnp.sum(jnp.where(wide_lanes == ex * 2 + l, table, 0.0), axis=1, keepdims=True)

    for l in range(2):
        need_weights(0, l)
        need_weights(1, l)

        @pl.loop(0, 2)
        def _(h):
            g = h * (l + 1)
            pre[l, h] = jnp.dot(rows[g, :, 0:width], wgu[l], preferred_element_type=f32)
            dots = jnp.dot(rows[g, :, width : 2 * width], wgu[l], preferred_element_type=f32)
            pre_gate, pre_up = pre[l, h, :, 0:half], pre[l, h, :, half:hid]
            gate_dot, up_dot = dots[:, 0:half], dots[:, half:hid]
            sig = jax.nn.sigmoid(pre_gate)
            silu = pre_gate * sig
            slope = sig * (1.0 + pre_gate * (1.0 - sig))
            hidden_tan = slope * gate_dot * pre_up + silu * up_dot
            mixed = gate_of(g, l, 128) * (silu * pre_up) + gate_of(g, l, 0) * hidden_tan
            mix[g, :, l * half : (l + 1) * half] = mixed.astype(bf)

    need_weights(2, 0)
    need_weights(2, 1)

    spans = [(0, hid), (0, half), (half, hid)]

    def down(g):
        lo, hi = spans[g]
        part[g] = jnp.dot(mix[g, :, lo:hi], wd[lo:hi, :], preferred_element_type=f32).astype(bf)

    image = send_home(down, part, cross, summed, far, landed, 0)
    image_ref[...] = image
    image_rows[0, slot_rows, :] = image.astype(bf)
    for copy in gather_finish(image_rows, 1, gather_start(image_rows, 1)):
        copy.wait_recv()

    def backward(g):
        lo, hi = spans[g]
        back = nt_dot(image_rows[g], wd[lo:hi, :])
        cots = jnp.zeros((n_rows, 128), f32)
        total = None
        for l in range(lo // half, hi // half):
            back_hidden = back[:, l * half - lo : (l + 1) * half - lo]
            h = 1 if g else 0
            pre_gate, pre_up = pre[l, h, :, 0:half], pre[l, h, :, half:hid]
            sig = jax.nn.sigmoid(pre_gate)
            silu = pre_gate * sig
            slope = sig * (1.0 + pre_gate * (1.0 - sig))
            cot = jnp.sum(back_hidden * (silu * pre_up), axis=1, keepdims=True)
            cots = cots + jnp.where(wide_lanes == ex * 2 + l, cot, 0.0)
            scaled = gate_of(g, l, 0) * back_hidden
            grads[l, :, 0:half] = (scaled * pre_up * slope).astype(bf)
            grads[l, :, half:hid] = (scaled * silu).astype(bf)
            term = nt_dot(grads[l], wgu[l])
            total = term if total is None else total + term
        part2[g, :, 0:width] = total.astype(bf)
        part2[g, :, width : width + 128] = cots.astype(bf)

    total = send_home(backward, part2, cross2, summed2, far2, landed2, 1)

    expert_grad = total[:, 0:width]
    cot = total[:, width : width + 128]
    prob = prob_keep[...]
    column_grad = prob * (cot - jnp.sum(prob * cot, axis=1, keepdims=True))
    high = column_grad.astype(bf)
    rest = column_grad - high.astype(f32)
    middle = rest.astype(bf)
    low = (rest - middle.astype(f32)).astype(bf)
    router = router_ref[...]
    router_grad = nt_dot(high, router) + (nt_dot(middle, router) + nt_dot(low, router))
    xfull = tok_ref[...].astype(f32)
    inv_rms = inv_keep[:, 0:1]
    pulled = gain_ref[...] * (expert_grad + router_grad)
    gram_ref[...] = inv_rms * pulled - xfull * (inv_rms * inv_rms * inv_rms) * jnp.mean(
        pulled * xfull, axis=1, keepdims=True
    )
    for copy in pending:
        copy.wait_send()


def on_device_dense(tokens, tangent, norm_gain, router, w_gate, w_up, w_down, routes):
    n_tok, width = tokens.shape
    hid = w_gate.shape[2]
    n_rows = 8 * n_tok
    bf, f32 = jnp.bfloat16, jnp.float32
    wide_router = jnp.pad(router, ((0, 0), (0, 128 - router.shape[1])))
    vm = pl.BlockSpec(memory_space=pltpu.VMEM)
    hbm = pl.BlockSpec(memory_space=pl.ANY)
    out = jax.ShapeDtypeStruct((n_tok, width), f32)
    dma = pltpu.SemaphoreType.DMA
    image, gram = pl.pallas_call(
        block_kernel,
        out_shape=(out, out),
        in_specs=[vm] * 5 + [hbm] * 3,
        out_specs=(vm, vm),
        scratch_shapes=[
            pltpu.VMEM((2, width, hid), bf),
            pltpu.VMEM((hid, width), bf),
            pltpu.VMEM((3, n_rows, 2 * width + 256), bf),
            pltpu.VMEM((2, 2, n_rows, hid), f32),
            pltpu.VMEM((3, n_rows, hid), bf),
            pltpu.VMEM((3, n_rows, width), bf),
            pltpu.VMEM((3, n_rows // 2, width), bf),
            pltpu.VMEM((3, n_rows // 2, width), bf),
            pltpu.VMEM((2, n_rows // 2, width), bf),
            pltpu.VMEM((4, n_tok, width), bf),
            pltpu.VMEM((3, n_rows, width), bf),
            pltpu.VMEM((2, n_rows, hid), bf),
            pltpu.VMEM((3, n_rows, width + 128), bf),
            pltpu.VMEM((3, n_rows // 2, width + 128), bf),
            pltpu.VMEM((3, n_rows // 2, width + 128), bf),
            pltpu.VMEM((2, n_rows // 2, width + 128), bf),
            pltpu.VMEM((4, n_tok, width + 128), bf),
            pltpu.VMEM((n_tok, 128), f32),
            pltpu.VMEM((n_tok, 128), f32),
            dma((3, 2, 3)), dma((3, 2, 3)), dma((3, 2)),
            dma((2, 3, 4)), dma((2, 3, 4)), dma((2, 6)), dma((2, 6)), dma((4, 3)), dma((4, 3)),
        ],
        compiler_params=pltpu.CompilerParams(
            collective_id=0, has_side_effects=True, vmem_limit_bytes=60 * 2**20
        ),
        cost_estimate=pl.CostEstimate(
            flops=2 * 16 * n_rows * width * hid, bytes_accessed=2**24, transcendentals=2**20
        ),
    )(tokens, tangent, norm_gain.reshape(1, width), wide_router, routes, w_gate, w_up, w_down)
    return image, gram


def solution(mesh):
    in_specs = (
        P(("dp", "expert"), None),
        P(("dp", "expert"), None),
        P(),
        P(),
        P("expert", "dp", None),
        P("expert", "dp", None),
        P("expert", None, "dp"),
        P(("dp", "expert"), None),
    )
    out_specs = (P(("dp", "expert"), None), P(("dp", "expert"), None))
    body = on_device
    if mesh.shape["dp"] == 4 and mesh.shape["expert"] == 8:
        body = on_device_dense
    return jax.shard_map(
        body, mesh=mesh, in_specs=in_specs, out_specs=out_specs, check_vma=False
    )
```

```python
import jax
import jax.numpy as jnp
from jax import lax
from jax.experimental import pallas as pl
from jax.experimental.pallas import tpu as pltpu
from jax.sharding import PartitionSpec as P

eps_value = 1e-06


def pick_columns(table, routes):
    hits = routes[:, :, None] == jnp.arange(table.shape[1], dtype=jnp.int32)[None, None, :]
    return jnp.sum(jnp.where(hits, table[:, None, :], jnp.zeros((), table.dtype)), axis=2)


def on_device(tokens, tangent, norm_gain, router, w_gate, w_up, w_down, routes):
    tok_rows, topk = routes.shape
    model_width = tokens.shape[1]
    experts_all = router.shape[1]
    local_experts = w_gate.shape[0]
    groups = lax.axis_size("expert")
    capacity = 2 * tok_rows * topk // experts_all
    xfull = tokens.astype(jnp.float32)
    vfull = tangent.astype(jnp.float32)
    inv_rms = lax.rsqrt(jnp.mean(xfull * xfull, axis=1, keepdims=True) + eps_value)
    normed = (norm_gain * xfull * inv_rms).astype(jnp.bfloat16)
    cross_term = jnp.mean(xfull * vfull, axis=1, keepdims=True)
    normed_tan = (norm_gain * (vfull * inv_rms - xfull * inv_rms**3 * cross_term)).astype(
        jnp.bfloat16
    )
    logits = jnp.dot(normed, router, preferred_element_type=jnp.float32)
    logit_tan = jnp.dot(normed_tan, router, preferred_element_type=jnp.float32)
    selected = pick_columns(logits, routes)
    sel_tan = pick_columns(logit_tan, routes)
    exp_sel = jnp.exp(selected)
    gate_prob = exp_sel / jnp.sum(exp_sel, axis=1, keepdims=True)
    gate_tan = gate_prob * (sel_tan - jnp.sum(gate_prob * sel_tan, axis=1, keepdims=True))
    gate_b = gate_prob.astype(jnp.bfloat16)
    gate_tan_b = gate_tan.astype(jnp.bfloat16)
    pair_count = tok_rows * topk
    flat_ids = routes.reshape(-1)
    order = jnp.arange(pair_count, dtype=jnp.int32)
    earlier = (flat_ids[None, :] == flat_ids[:, None]) & (order[None, :] < order[:, None])
    slot_rank = jnp.sum(earlier.astype(jnp.int32), axis=1)
    slot_of_pair = flat_ids * capacity + slot_rank
    slot_hits = slot_of_pair[None, :] == jnp.arange(experts_all * capacity, dtype=jnp.int32)[:, None]
    slot_table = jnp.max(
        jnp.where(slot_hits, jnp.arange(pair_count, dtype=jnp.int32)[None, :], -1), axis=1
    )
    slot_valid = slot_table >= 0
    safe_pair = jnp.maximum(slot_table, 0)
    tok_idx = safe_pair // topk
    which_k = safe_pair % topk
    bf_zero = jnp.zeros((), jnp.bfloat16)
    send_rows = jnp.stack(
        (
            jnp.where(slot_valid[:, None], normed[tok_idx], bf_zero),
            jnp.where(slot_valid[:, None], normed_tan[tok_idx], bf_zero),
        )
    )
    send_rows = send_rows.reshape(2, groups, local_experts * capacity, model_width)
    send_gates = jnp.stack(
        (
            jnp.where(slot_valid, gate_b[tok_idx, which_k], bf_zero),
            jnp.where(slot_valid, gate_tan_b[tok_idx, which_k], bf_zero),
        )
    )
    send_gates = send_gates.reshape(2, groups, local_experts * capacity)
    recv_rows, recv_gates = (
        lax.all_to_all(send_rows, "expert", split_axis=1, concat_axis=1, tiled=True),
        lax.all_to_all(send_gates, "expert", split_axis=1, concat_axis=1, tiled=True),
    )
    slot_rows = recv_rows.reshape(2, groups, local_experts, capacity, model_width)
    recv_gates = recv_gates.reshape(2, groups, local_experts, capacity).astype(jnp.float32)
    gate_val = recv_gates[0][..., None]
    tan_val = recv_gates[1][..., None]
    gate_full, up_full, down_full = (
        lax.all_gather(w_gate, "dp", axis=1, tiled=True),
        lax.all_gather(w_up, "dp", axis=1, tiled=True),
        lax.all_gather(w_down, "dp", axis=2, tiled=True),
    )
    pre_both = jnp.einsum(
        "tslkd,ldf->tslkf", slot_rows, gate_full, preferred_element_type=jnp.float32
    )
    up_both = jnp.einsum("tslkd,ldf->tslkf", slot_rows, up_full, preferred_element_type=jnp.float32)
    pre_gate = pre_both[0]
    gate_dot = pre_both[1]
    pre_up = up_both[0]
    up_dot = up_both[1]
    sig_gate = jax.nn.sigmoid(pre_gate)
    silu_gate = pre_gate * sig_gate
    slope_gate = sig_gate * (1.0 + pre_gate * (1.0 - sig_gate))
    hidden = silu_gate * pre_up
    hidden_tan = slope_gate * gate_dot * pre_up + silu_gate * up_dot
    mixed_rows = (tan_val * hidden + gate_val * hidden_tan).astype(jnp.bfloat16)
    pair_image = jnp.einsum(
        "slkf,lfd->slkd", mixed_rows, down_full, preferred_element_type=jnp.float32
    )
    pair_send = pair_image.astype(jnp.bfloat16).reshape(
        groups, local_experts * capacity, model_width
    )
    pair_back = lax.all_to_all(pair_send, "expert", split_axis=0, concat_axis=0, tiled=True)
    pair_back = pair_back.reshape(experts_all * capacity, model_width)
    tangent_image = jnp.sum(
        pair_back[slot_of_pair].astype(jnp.float32).reshape(tok_rows, topk, model_width), axis=1
    )
    image_b = tangent_image.astype(jnp.bfloat16)
    send_cot = jnp.where(slot_valid[:, None], image_b[tok_idx], bf_zero).reshape(
        groups, local_experts * capacity, model_width
    )
    recv_cot = lax.all_to_all(send_cot, "expert", split_axis=0, concat_axis=0, tiled=True)
    recv_cot = recv_cot.reshape(groups, local_experts, capacity, model_width)
    back_hidden = jnp.einsum(
        "slkd,lfd->slkf", recv_cot, down_full, preferred_element_type=jnp.float32
    )
    gate_cot = jnp.sum(back_hidden * hidden, axis=3).astype(jnp.bfloat16)
    scaled = gate_val * back_hidden
    grad_gate = (scaled * pre_up * slope_gate).astype(jnp.bfloat16)
    grad_up = (scaled * silu_gate).astype(jnp.bfloat16)
    pair_grad = jnp.einsum(
        "slkf,ldf->slkd", grad_gate, gate_full, preferred_element_type=jnp.float32
    )
    pair_grad = pair_grad + jnp.einsum(
        "slkf,ldf->slkd", grad_up, up_full, preferred_element_type=jnp.float32
    )
    grad_send = pair_grad.astype(jnp.bfloat16).reshape(
        groups, local_experts * capacity, model_width
    )
    cot_send = gate_cot.reshape(groups, local_experts * capacity)
    grad_back, cot_back = (
        lax.all_to_all(grad_send, "expert", split_axis=0, concat_axis=0, tiled=True),
        lax.all_to_all(cot_send, "expert", split_axis=0, concat_axis=0, tiled=True),
    )
    grad_back = grad_back.reshape(experts_all * capacity, model_width)
    cot_back = cot_back.reshape(experts_all * capacity)
    expert_grad = jnp.sum(
        grad_back[slot_of_pair].astype(jnp.float32).reshape(tok_rows, topk, model_width), axis=1
    )
    pair_cot = cot_back[slot_of_pair].astype(jnp.float32).reshape(tok_rows, topk)
    logit_grad = gate_prob * (pair_cot - jnp.sum(gate_prob * pair_cot, axis=1, keepdims=True))
    hits = routes[:, :, None] == jnp.arange(experts_all, dtype=jnp.int32)[None, None, :]
    column_grad = jnp.sum(jnp.where(hits, logit_grad[:, :, None], 0.0), axis=1)
    router_grad = jnp.dot(
        column_grad, router.astype(jnp.float32).T, precision=lax.Precision.HIGHEST
    )
    pulled = norm_gain * (expert_grad + router_grad)
    gram_image = inv_rms * pulled - xfull * inv_rms**3 * jnp.mean(
        pulled * xfull, axis=1, keepdims=True
    )
    return (tangent_image, gram_image)


MESH = pl.DeviceIdType.MESH


def nt_dot(left, right):
    return lax.dot_general(
        left, right, (((1,), (1,)), ((), ())), preferred_element_type=jnp.float32
    )


def block_kernel(
    tok_ref, tan_ref, gain_ref, router_ref, routes_ref, wg_ref, wu_ref, wd_ref,
    image_ref, gram_ref,
    wgu, wd, rows, pre, mix, part, cross, summed, far, landed, image_rows,
    grads, part2, cross2, summed2, far2, landed2, prob_keep, inv_keep,
    w_send, w_recv, w_own, a_send, a_recv, r_send, r_recv, c_send, c_recv,
):
    f32, bf = jnp.float32, jnp.bfloat16
    n_tok, width = tok_ref.shape
    slab, hid = wg_ref.shape[1], wg_ref.shape[2]
    half = hid // 2
    n_core = 4 * n_tok
    dp, ex = lax.axis_index("dp"), lax.axis_index("expert")
    y, x = dp // 2, dp % 2
    z, core = ex // 2, ex % 2
    other = 1 - core
    x_peer = (y * 2 + 1 - x, ex)
    y_peer = ((1 - y) * 2 + x, ex)
    mate = (dp, z * 2 + other)
    z_peers = [(dp, (z + dz) % 4 * 2 + core) for dz in range(1, 4)]
    core_rows = pl.ds(pl.multiple_of(core * n_core, n_core), n_core)
    other_rows = pl.ds(pl.multiple_of(other * n_core, n_core), n_core)

    def block_rows(dz):
        return pl.ds(pl.multiple_of(core * n_core + (z + dz) % 4 * n_tok, n_tok), n_tok)

    def z_rows(dz):
        return pl.ds(pl.multiple_of((z + dz) % 4 * n_tok, n_tok), n_tok)

    slot_rows = block_rows(0)

    barrier = pltpu.get_barrier_semaphore()
    friends = z_peers + [x_peer, y_peer, mate]
    for friend in friends:
        pl.semaphore_signal(barrier, inc=1, device_id=friend, device_id_type=MESH)
    pl.semaphore_wait(barrier, len(friends))

    pending = []

    def push(src, dst, sems, where, device):
        copy = pltpu.make_async_remote_copy(
            src_ref=src, dst_ref=dst, send_sem=sems[0].at[where], recv_sem=sems[1].at[where],
            device_id=device, device_id_type=MESH,
        )
        copy.start()
        pending.append(copy)
        return copy

    def slab_of(index):
        return pl.ds(pl.multiple_of(index * slab, slab), slab)

    def weight_dst(kind, l, index):
        if kind == 2:
            return wd.at[pl.ds(l * half, half), slab_of(index)]
        return wgu.at[l, slab_of(index), pl.ds(kind * half, half)]

    def weight_src(kind, l, which):
        part_of = pl.ds(pl.multiple_of(which * half, half), half)
        if kind == 2:
            return wd_ref.at[l, part_of, :]
        return (wg_ref, wu_ref)[kind].at[l, :, part_of]

    moving, relayed = {}, {}
    w_sems = (w_send, w_recv)

    def start_weights(kind, l):
        mine = weight_dst(kind, l, dp)
        for_x, for_y = (1 - x, x) if l == 0 else (y, 1 - y)
        own = pltpu.make_async_copy(
            weight_src(kind, l, x if l == 0 else y), mine, w_own.at[kind, l]
        )
        ends = [(for_x, 0, x_peer), (for_y, 1, y_peer)]
        copies = [
            push(weight_src(kind, l, which), mine, w_sems, (kind, l, p), peer)
            for which, p, peer in ends
        ]
        own.start()
        moving[kind, l] = (copies, own)

    def relay_weights(kind, l):
        moving[kind, l][0][l].wait_recv()
        if l == 0:
            block = weight_dst(kind, l, y * 2 + 1 - x)
            relayed[kind, l] = push(block, block, w_sems, (kind, l, 2), y_peer)
        else:
            block = weight_dst(kind, l, (1 - y) * 2 + x)
            relayed[kind, l] = push(block, block, w_sems, (kind, l, 2), x_peer)

    def need_weights(kind, l):
        copies, own = moving[kind, l]
        own.wait()
        copies[1 - l].wait_recv()
        relayed[kind, l].wait_recv()

    a_sems, c_sems, r_sems = (a_send, a_recv), (c_send, c_recv), (r_send, r_recv)

    def gather_start(buf, turn):
        mine = buf.at[0, slot_rows]
        along_z = [
            push(mine, mine, a_sems, (turn, 0, i + 1), peer) for i, peer in enumerate(z_peers)
        ]
        sides = [
            {0: push(mine, buf.at[1 + s, slot_rows], a_sems, (turn, 1 + s, 0), peer)}
            for s, peer in enumerate((x_peer, y_peer))
        ]
        return along_z, sides, [push(mine, mine, c_sems, (turn, 0), mate)]

    def gather_finish(buf, turn, started):
        along_z, sides, to_mate = started
        for dz in (3, 1, 2):
            along_z[dz - 1].wait_recv()
            got = block_rows(4 - dz)
            block = buf.at[0, got]
            for s, peer in enumerate((x_peer, y_peer)):
                sides[s][dz] = push(
                    block, buf.at[1 + s, got], a_sems, (turn, 1 + s, dz), peer
                )
            to_mate.append(push(block, block, c_sems, (turn, dz), mate))
        for dz in (0, 3, 1, 2):
            for s in range(2):
                sides[s][dz].wait_recv()
                block = buf.at[1 + s, block_rows((4 - dz) % 4)]
                to_mate.append(push(block, block, c_sems, (turn, 4 + 4 * s + dz), mate))
        return to_mate

    def send_home(compute, parts, crossed, mid, far, land, turn):
        over, aside = {}, {}

        def to_mate(g):
            over[g] = push(
                parts.at[g, other_rows], crossed.at[g], c_sems, (2 + turn, g), mate
            )

        def add_mate(g):
            over[g].wait_recv()
            mid[g] = (parts[g, core_rows, :].astype(f32) + crossed[g].astype(f32)).astype(bf)

        def to_side(g, peer):
            add_mate(g)
            for dz in (2, 1, 3, 0):
                aside[g, dz] = push(
                    mid.at[g, z_rows(dz)], far.at[g - 1, z_rows(dz)],
                    r_sems, (turn, 4 * g + dz), peer,
                )

        compute(1)
        to_mate(1)
        compute(2)
        to_mate(2)
        to_side(1, x_peer)
        to_side(2, y_peer)
        compute(0)
        to_mate(0)
        over[0].wait_recv()
        copies = {}
        for dz in (2, 1, 3, 0):
            aside[1, dz].wait_recv()
            aside[2, dz].wait_recv()
            at = z_rows(dz)
            own = parts[0, block_rows(dz), :].astype(f32) + crossed[0, at, :].astype(f32)
            total = own + (far[0, at, :].astype(f32) + far[1, at, :].astype(f32))
            if dz:
                mid[0, at, :] = total.astype(bf)
                copies[dz] = push(
                    mid.at[0, at], land.at[z], r_sems, (turn, dz), z_peers[dz - 1]
                )
        for dz in (1, 3, 2):
            copies[dz].wait_recv()
            total = total + land[(z + 4 - dz) % 4].astype(f32)
        return total

    start_weights(0, 0)

    xfull = tok_ref[...].astype(f32)
    vfull = tan_ref[...].astype(f32)
    gain = gain_ref[...]
    inv_rms = lax.rsqrt(jnp.mean(xfull * xfull, axis=1, keepdims=True) + eps_value)
    normed = (gain * xfull * inv_rms).astype(bf)
    cross_term = jnp.mean(xfull * vfull, axis=1, keepdims=True)
    inv_cube = inv_rms * inv_rms * inv_rms
    normed_tan = (gain * (vfull * inv_rms - xfull * inv_cube * cross_term)).astype(bf)
    rows[0, slot_rows, 0:width] = normed
    rows[0, slot_rows, width : 2 * width] = normed_tan
    logits = jnp.dot(normed, router_ref[...], preferred_element_type=f32)
    logit_tan = jnp.dot(normed_tan, router_ref[...], preferred_element_type=f32)
    lanes = lax.broadcasted_iota(jnp.int32, (n_tok, 128), 1)
    chosen = jnp.zeros((n_tok, 128), f32)
    for k in range(routes_ref.shape[1]):
        chosen = chosen + jnp.where(lanes == routes_ref[:, k : k + 1], 1.0, 0.0)
    exp_sel = jnp.where(chosen > 0.5, jnp.exp(logits), 0.0)
    gate_prob = exp_sel / jnp.sum(exp_sel, axis=1, keepdims=True)
    gate_tan = gate_prob * (
        logit_tan - jnp.sum(gate_prob * logit_tan, axis=1, keepdims=True)
    )
    rows[0, slot_rows, 2 * width : 2 * width + 128] = gate_prob.astype(bf)
    rows[0, slot_rows, 2 * width + 128 : 2 * width + 256] = gate_tan.astype(bf)
    prob_keep[...] = gate_prob
    inv_keep[...] = jnp.broadcast_to(inv_rms, (n_tok, 128))

    started = gather_start(rows, 0)
    pieces = [(0, 0), (1, 0), (0, 1), (1, 1), (2, 0), (2, 1)]
    for kind, l in pieces[1:]:
        start_weights(kind, l)
    for copy in gather_finish(rows, 0, started):
        copy.wait_recv()
    for kind, l in pieces:
        relay_weights(kind, l)

    n_rows = rows.shape[1]
    wide_lanes = lax.broadcasted_iota(jnp.int32, (n_rows, 128), 1)

    def gate_of(part_no, l, offset):
        table = rows[part_no, :, 2 * width + offset : 2 * width + offset + 128].astype(f32)
        return jnp.sum(jnp.where(wide_lanes == ex * 2 + l, table, 0.0), axis=1, keepdims=True)

    for l in range(2):
        need_weights(0, l)
        need_weights(1, l)

        @pl.loop(0, 2)
        def _(h):
            g = h * (l + 1)
            pre[l, h] = jnp.dot(rows[g, :, 0:width], wgu[l], preferred_element_type=f32)
            dots = jnp.dot(rows[g, :, width : 2 * width], wgu[l], preferred_element_type=f32)
            pre_gate, pre_up = pre[l, h, :, 0:half], pre[l, h, :, half:hid]
            gate_dot, up_dot = dots[:, 0:half], dots[:, half:hid]
            sig = jax.nn.sigmoid(pre_gate)
            silu = pre_gate * sig
            slope = sig * (1.0 + pre_gate * (1.0 - sig))
            hidden_tan = slope * gate_dot * pre_up + silu * up_dot
            mixed = gate_of(g, l, 128) * (silu * pre_up) + gate_of(g, l, 0) * hidden_tan
            mix[g, :, l * half : (l + 1) * half] = mixed.astype(bf)

    need_weights(2, 0)
    need_weights(2, 1)

    spans = [(0, hid), (0, half), (half, hid)]

    def down(g):
        lo, hi = spans[g]
        part[g] = jnp.dot(mix[g, :, lo:hi], wd[lo:hi, :], preferred_element_type=f32).astype(bf)

    image = send_home(down, part, cross, summed, far, landed, 0)
    image_ref[...] = image
    image_rows[0, slot_rows, :] = image.astype(bf)
    for copy in gather_finish(image_rows, 1, gather_start(image_rows, 1)):
        copy.wait_recv()

    def backward(g):
        lo, hi = spans[g]
        back = nt_dot(image_rows[g], wd[lo:hi, :])
        cots = jnp.zeros((n_rows, 128), f32)
        total = None
        for l in range(lo // half, hi // half):
            back_hidden = back[:, l * half - lo : (l + 1) * half - lo]
            h = 1 if g else 0
            pre_gate, pre_up = pre[l, h, :, 0:half], pre[l, h, :, half:hid]
            sig = jax.nn.sigmoid(pre_gate)
            silu = pre_gate * sig
            slope = sig * (1.0 + pre_gate * (1.0 - sig))
            cot = jnp.sum(back_hidden * (silu * pre_up), axis=1, keepdims=True)
            cots = cots + jnp.where(wide_lanes == ex * 2 + l, cot, 0.0)
            scaled = gate_of(g, l, 0) * back_hidden
            grads[l, :, 0:half] = (scaled * pre_up * slope).astype(bf)
            grads[l, :, half:hid] = (scaled * silu).astype(bf)
            term = nt_dot(grads[l], wgu[l])
            total = term if total is None else total + term
        part2[g, :, 0:width] = total.astype(bf)
        part2[g, :, width : width + 128] = cots.astype(bf)

    total = send_home(backward, part2, cross2, summed2, far2, landed2, 1)

    expert_grad = total[:, 0:width]
    cot = total[:, width : width + 128]
    prob = prob_keep[...]
    column_grad = prob * (cot - jnp.sum(prob * cot, axis=1, keepdims=True))
    high = column_grad.astype(bf)
    rest = column_grad - high.astype(f32)
    middle = rest.astype(bf)
    low = (rest - middle.astype(f32)).astype(bf)
    router = router_ref[...]
    router_grad = nt_dot(high, router) + (nt_dot(middle, router) + nt_dot(low, router))
    xfull = tok_ref[...].astype(f32)
    inv_rms = inv_keep[:, 0:1]
    pulled = gain_ref[...] * (expert_grad + router_grad)
    gram_ref[...] = inv_rms * pulled - xfull * (inv_rms * inv_rms * inv_rms) * jnp.mean(
        pulled * xfull, axis=1, keepdims=True
    )
    for copy in pending:
        copy.wait_send()


def on_device_dense(tokens, tangent, norm_gain, router, w_gate, w_up, w_down, routes):
    n_tok, width = tokens.shape
    hid = w_gate.shape[2]
    n_rows = 8 * n_tok
    bf, f32 = jnp.bfloat16, jnp.float32
    wide_router = jnp.pad(router, ((0, 0), (0, 128 - router.shape[1])))
    vm = pl.BlockSpec(memory_space=pltpu.VMEM)
    hbm = pl.BlockSpec(memory_space=pl.ANY)
    out = jax.ShapeDtypeStruct((n_tok, width), f32)
    dma = pltpu.SemaphoreType.DMA
    image, gram = pl.pallas_call(
        block_kernel,
        out_shape=(out, out),
        in_specs=[vm] * 5 + [hbm] * 3,
        out_specs=(vm, vm),
        scratch_shapes=[
            pltpu.VMEM((2, width, hid), bf),
            pltpu.VMEM((hid, width), bf),
            pltpu.VMEM((3, n_rows, 2 * width + 256), bf),
            pltpu.VMEM((2, 2, n_rows, hid), f32),
            pltpu.VMEM((3, n_rows, hid), bf),
            pltpu.VMEM((3, n_rows, width), bf),
            pltpu.VMEM((3, n_rows // 2, width), bf),
            pltpu.VMEM((3, n_rows // 2, width), bf),
            pltpu.VMEM((2, n_rows // 2, width), bf),
            pltpu.VMEM((4, n_tok, width), bf),
            pltpu.VMEM((3, n_rows, width), bf),
            pltpu.VMEM((2, n_rows, hid), bf),
            pltpu.VMEM((3, n_rows, width + 128), bf),
            pltpu.VMEM((3, n_rows // 2, width + 128), bf),
            pltpu.VMEM((3, n_rows // 2, width + 128), bf),
            pltpu.VMEM((2, n_rows // 2, width + 128), bf),
            pltpu.VMEM((4, n_tok, width + 128), bf),
            pltpu.VMEM((n_tok, 128), f32),
            pltpu.VMEM((n_tok, 128), f32),
            dma((3, 2, 3)), dma((3, 2, 3)), dma((3, 2)),
            dma((2, 3, 4)), dma((2, 3, 4)), dma((2, 12)), dma((2, 12)), dma((4, 12)), dma((4, 12)),
        ],
        compiler_params=pltpu.CompilerParams(
            collective_id=0, has_side_effects=True, vmem_limit_bytes=60 * 2**20
        ),
        cost_estimate=pl.CostEstimate(
            flops=2 * 16 * n_rows * width * hid, bytes_accessed=2**24, transcendentals=2**20
        ),
    )(tokens, tangent, norm_gain.reshape(1, width), wide_router, routes, w_gate, w_up, w_down)
    return image, gram


def solution(mesh):
    in_specs = (
        P(("dp", "expert"), None),
        P(("dp", "expert"), None),
        P(),
        P(),
        P("expert", "dp", None),
        P("expert", "dp", None),
        P("expert", None, "dp"),
        P(("dp", "expert"), None),
    )
    out_specs = (P(("dp", "expert"), None), P(("dp", "expert"), None))
    body = on_device
    if mesh.shape["dp"] == 4 and mesh.shape["expert"] == 8:
        body = on_device_dense
    return jax.shard_map(
        body, mesh=mesh, in_specs=in_specs, out_specs=out_specs, check_vma=False
    )
```
